128 devices in a mesh: table: 32 (over z, x, core), code: 4 (over y).
Axes of the slice: x: 4, y: 4, z: 4, core: 2. Of those that a mesh axis runs over, the one named last changes fastest.
Arguments:
- pooled_grad: bfloat16 [32, 4, 2048, 128], P('table', 'code'), may hold values from -6 to 6
- bag_rows: int32 [32, 4, 32, 4, 2048], P('table', 'code'), may hold values from 0 to 511
- dest_blocks: int32 [32, 4, 32, 4], P('table', 'code'), may hold values from 0 to 95
- block_counts: int32 [32, 4, 32], P('table', 'code'), may hold values from 1 to 4, as said below
- table: float32 [32, 4, 96, 128, 128], P('table', 'code'), may hold values from -4 to 4
- accum: float32 [32, 4, 96, 128], P('table', 'code'), may hold values from 0.1 to 10
- parity: float32 [32, 96, 128, 128], P('table', 'code'), may hold values from -6 to 6
- parity_slot: int32 [32, 4, 96], P('table', 'code'), may hold values from 0 to 95, each once within a row
Outputs:
- new_table: float32 [32, 4, 96, 128, 128], P('table', 'code')
- new_accum: float32 [32, 4, 96, 128], P('table', 'code')
- new_parity: float32 [32, 96, 128, 128], P('table', 'code')
The draws below stay inside these ranges and needn't reach their ends.
Inputs may be any that keep to these rules, and one draw needn't show every extreme that they name: `bag_rows`: A value r < 128 puts the sample into row r of the slot's block; larger values put it into none. `dest_blocks`: entries at slots k >= block_counts of that owner are ignored. Slots k >= block_counts[t, c, o] carry no block, and their entries of bag_rows and dest_blocks are ignored. For every index of the code axis some owner receives 4 blocks from every device of that index.
All inputs are finite; a program needn't handle non-finite values.
Results may differ from the reference program's by a relative error of at most 0.0015.
Values may be sent and summed in bfloat16 or wider, within the bound.
A program may use at most 128 MiB of HBM per device.

```python
import math
import jax
import jax.numpy as jnp
from jax import lax

E = 128
BLK = 128
CAP = 4
BATCH = 2048
BLOCKS_DEV = 96
OWNERS = 32
CODERS = 4


def draw_block_counts(key, part):
    key = jax.random.fold_in(key, 7)
    first_key, second_key = jax.random.split(key)
    member_keys = jax.random.split(first_key, CODERS)

    def owner_order(member_key):
        return jax.random.permutation(member_key, OWNERS).astype(jnp.int32)
    orders = jax.vmap(owner_order)(member_keys)
    owner_ids = jnp.arange(OWNERS, dtype=jnp.int32)
    hot_owner = (owner_ids[None, :] == orders[:, 0:1]) | (owner_ids[None, :] == orders[:, 1:2])
    base_counts = jax.random.randint(second_key, (OWNERS, CODERS, OWNERS), 1, 5, dtype=jnp.int32)
    return jnp.where(hot_owner[None, :, :], CAP, jnp.minimum(base_counts, CAP)).astype(jnp.int32)


def with_ends(drawn, stream_key, least, largest):
    longest = drawn.shape.index(max(drawn.shape))
    spots = []
    for shift in (0, 1):
        where = [jax.random.randint(jax.random.fold_in(stream_key, axis), (), 0, length) for axis, length in enumerate(drawn.shape)]
        where[longest] = (where[longest] + shift) % drawn.shape[longest]
        spots.append(tuple(where))
    return drawn.at[spots[0]].set(least).at[spots[1]].set(largest)


def block_levels(key, shape, cuts, smallest, high):
    def one(axis_at, shards_of):
        heights = jax.random.uniform(jax.random.fold_in(jax.random.fold_in(key, 6), axis_at), (shards_of,), jnp.float32, smallest / len(cuts), high / len(cuts))
        return jnp.repeat(jnp.exp(heights), shape[axis_at] // shards_of).reshape((-1,) + (1,) * (len(shape) - axis_at - 1))

    level = one(*cuts[0])
    for cut in cuts[1:]:
        level = level * one(*cut)
    return level


def normal_values(key, dims, spread, bound, cuts=(), held_as=jnp.bfloat16):
    values = jax.random.normal(key, dims, jnp.float32) * spread
    if len(cuts) > 0:
        values = block_levels(key, dims, cuts, -0.22, 0.18) * values
    return jnp.clip(values, min=-bound, max=bound).astype(held_as)


def setup_inputs(seed: int = 0) -> dict:
    seeds = jax.random.split(jax.random.key(seed), 9)
    pooled_grad = normal_values(seeds[0], (OWNERS, CODERS, BATCH, E), 1.0, 6.0, ((0, 32), (1, 4)))
    bag_rows = with_ends(jax.random.randint(seeds[1], (OWNERS, CODERS, OWNERS, CAP, BATCH), 0, 4 * BLK), jax.random.fold_in(seeds[1], 1), 0, (4 * BLK) - 1).astype(jnp.int32)
    dest_blocks = with_ends(jax.random.randint(seeds[2], (OWNERS, CODERS, OWNERS, CAP), 0, BLOCKS_DEV), jax.random.fold_in(seeds[2], 1), 0, BLOCKS_DEV - 1).astype(jnp.int32)
    block_counts = draw_block_counts(jax.random.fold_in(seeds[8], 71), 0)
    table = normal_values(seeds[4], (OWNERS, CODERS, BLOCKS_DEV, BLK, E), 0.5, 4.0, ((0, 32), (1, 4)), jnp.float32)
    accum = jnp.clip(jnp.exp(math.log(10.0) - 4.6051702 * jax.random.uniform(seeds[5], (OWNERS, CODERS, BLOCKS_DEV, BLK), jnp.float32) ** block_levels(seeds[5], (OWNERS, CODERS, BLOCKS_DEV, BLK), ((0, 32), (1, 4)), -0.2, 0.2)), 0.1, 10.0)
    parity = normal_values(seeds[6], (OWNERS, BLOCKS_DEV, BLK, E), 1.0, 6.0, ((0, 32), (1, 4)), jnp.float32)
    parity_slot = jax.vmap(lambda own: jax.random.permutation(own, BLOCKS_DEV))(jax.random.split(seeds[7], OWNERS * CODERS)).reshape((OWNERS, CODERS, BLOCKS_DEV)).astype(jnp.int32)
    return dict(pooled_grad=pooled_grad, bag_rows=bag_rows, dest_blocks=dest_blocks, block_counts=block_counts, table=table, accum=accum, parity=parity, parity_slot=parity_slot)


LEARN_RATE = 0.2

def reference(pooled_grad, bag_rows, dest_blocks, block_counts, table, accum, parity, parity_slot):
    senders = OWNERS * CODERS
    pooled_all = pooled_grad.reshape(senders, BATCH, E)
    bag_lists = bag_rows.reshape(senders, OWNERS, CAP, BATCH)
    dest_lists = dest_blocks.reshape(senders, OWNERS, CAP)
    count_lists = block_counts.reshape(senders, OWNERS)
    row_ids = jnp.arange(BLK, dtype=jnp.int32)
    slot_ids = jnp.arange(CAP, dtype=jnp.int32)
    owner_ids = jnp.broadcast_to(jnp.arange(OWNERS, dtype=jnp.int32)[:, None], (OWNERS, CAP))

    def add_sender(grad_total, sender_item):
        sender_index, one_pooled, one_bags, one_dests, one_counts = sender_item
        onehot = (one_bags[:, :, None, :] == row_ids[None, None, :, None]).astype(jnp.float32)
        slot_terms = jnp.einsum('okrs,se->okre', onehot, one_pooled.astype(jnp.float32), precision=lax.Precision.HIGHEST)
        live_mask = slot_ids[None, :] < one_counts[:, None]
        slot_terms = jnp.where(live_mask[:, :, None, None], slot_terms, 0.0)
        rounded = lax.optimization_barrier(slot_terms.astype(jnp.bfloat16))
        code_index = (sender_index % CODERS).astype(jnp.int32)
        grad_total = grad_total.at[owner_ids, code_index, one_dests.astype(jnp.int32)].add(rounded.astype(jnp.float32))
        return (grad_total, None)
    start_total = jnp.zeros((OWNERS, CODERS, BLOCKS_DEV, BLK, E), jnp.float32)
    sender_range = jnp.arange(senders, dtype=jnp.int32)
    grad_total, _ = lax.scan(add_sender, start_total, (sender_range, pooled_all, bag_lists, dest_lists, count_lists))
    row_grad = lax.optimization_barrier(grad_total.astype(jnp.bfloat16))
    grad_float = row_grad.astype(jnp.float32)
    new_accum = accum + lax.optimization_barrier(jnp.mean(grad_float * grad_float, axis=-1))
    row_delta = -LEARN_RATE * grad_float * lax.rsqrt(new_accum)[..., None]
    new_table = table + row_delta
    position_order = jnp.argsort(parity_slot, axis=-1).astype(jnp.int32)
    placed = jnp.take_along_axis(row_delta, position_order[:, :, :, None, None], axis=2)
    new_parity = parity + lax.optimization_barrier(jnp.sum(placed, axis=1))
    return (new_table, new_accum, new_parity)
```

```python
import jax
import jax.numpy as jnp
from jax import lax
from jax.experimental import pallas as pl
from jax.experimental.pallas import tpu as pltpu
from jax.sharding import PartitionSpec as P

LEARN_RATE = 0.2
MESH = pl.DeviceIdType.MESH

RING = 4
CORES = 2
OWNERS = RING * RING * CORES
CODERS = 4
CAP = 4
E = 128
BLK = 128
BLOCKS = 96
HELD = BLOCKS // CODERS
BATCH = 2048

ROWS = 16
CHUNKS = BLK // ROWS
GROUP = 8
PARITY_GROUP = 32
LAG = 3
SLOT_ROWS = CAP * ROWS
PAIRS = OWNERS // 2


def send_order():
    offsets = [(dz, dx, dc) for dz in range(RING) for dx in range(RING) for dc in range(CORES)][1:]
    offsets.sort(key=lambda m: -(min(m[0], RING - m[0]) + min(m[1], RING - m[1])))
    order = []
    for dz, dx, dc in offsets:
        for _ in range(4):
            if (dz, dx, dc) not in order:
                order.append((dz, dx, dc))
            dz, dx = dx, (RING - dz) % RING
    return order


ORDER = send_order()
PEERS = len(ORDER)


def kernel(
    pooled_hbm, bags_hbm, dest_ref, count_ref, table_hbm, accum_ref, parity_hbm, slot_ref,
    table_out, accum_out, parity_out,
    pooled, bags, id_send, id_recv, sent, received, selector, table, parity, accum_t, new_accum_t,
    delta, delta_send, delta_recv,
    in_sem, id_send_sem, id_recv_sem, send_sem, recv_sem, own_sem, delta_send_sem, delta_recv_sem,
    table_sem, parity_sem,
):
    me = lax.axis_index("table")
    code = lax.axis_index("code")
    z, x, core = me // (RING * CORES), (me // CORES) % RING, me % CORES

    def owner_at(offset):
        dz, dx, dc = offset
        return (((z + dz) % RING) * RING + (x + dx) % RING) * CORES + (core + dc) % CORES

    barrier = pltpu.get_barrier_semaphore()
    for offset in ORDER:
        pl.semaphore_signal(barrier, inc=1, device_id=(owner_at(offset), code), device_id_type=MESH)
    for step in range(1, CODERS):
        pl.semaphore_signal(barrier, inc=1, device_id=(me, (code + step) % CODERS), device_id_type=MESH)

    loads = [
        pltpu.make_async_copy(pooled_hbm, pooled, in_sem.at[0]),
        pltpu.make_async_copy(bags_hbm, bags, in_sem.at[1]),
        pltpu.make_async_copy(table_hbm, table, in_sem.at[2]),
        pltpu.make_async_copy(parity_hbm, parity, in_sem.at[3]),
    ]
    for load in loads:
        load.start()

    lane = lax.broadcasted_iota(jnp.int32, (1, E), 1)
    lane_slot = (lane // ROWS) % CAP
    for owner in range(OWNERS):
        ids = jnp.full((1, E), -1, jnp.int32)
        for k in range(CAP):
            ids = jnp.where((lane_slot == k) & (k < count_ref[0, owner]), dest_ref[k, owner], ids)
        id_send[owner] = ids

    slot_lanes = jnp.full((1, E), -1, jnp.int32)
    for b in range(BLOCKS):
        slot_lanes = jnp.where(lane == b, slot_ref[0, b], slot_lanes)

    padding = jnp.zeros((BLK - BLOCKS, BLK), jnp.float32)
    accum_t[...] = jnp.concatenate([accum_ref[...], padding], axis=0).T
    new_accum_t[...] = jnp.zeros_like(new_accum_t)

    loads[0].wait()
    loads[1].wait()

    def slot_terms(q):
        row_index = lax.broadcasted_iota(jnp.int32, (ROWS, E), 0) + q * ROWS

        def group_terms(g, carry):
            tiles = []
            for j in range(GROUP):
                owner = g * GROUP + j
                for k in range(CAP):
                    wanted = jnp.where(k < count_ref[0, owner], row_index, -1)
                    wanted = jnp.concatenate([wanted] * (BATCH // E), axis=1)
                    bag = bags[owner, pl.ds(k, 1), :]
                    tiles.append(jnp.where(bag == wanted, 1.0, 0.0).astype(jnp.bfloat16))
            onehot = jnp.concatenate(tiles, axis=0)
            sums = jnp.dot(onehot, pooled[...], preferred_element_type=jnp.float32)
            sent[q, pl.ds(g * GROUP, GROUP)] = sums.astype(jnp.bfloat16).reshape(GROUP, SLOT_ROWS, E)
            return carry

        lax.fori_loop(0, OWNERS // GROUP, group_terms, 0)

    def send_ids():
        for i, offset in enumerate(ORDER):
            owner = owner_at(offset)
            pltpu.make_async_remote_copy(
                src_ref=id_send.at[owner], dst_ref=id_recv.at[i],
                send_sem=id_send_sem, recv_sem=id_recv_sem,
                device_id=(owner, code), device_id_type=MESH,
            ).start()

    def send_chunk(q):
        for i, offset in enumerate(ORDER):
            owner = owner_at(offset)
            pltpu.make_async_remote_copy(
                src_ref=sent.at[q, owner], dst_ref=received.at[q, i],
                send_sem=send_sem.at[q], recv_sem=recv_sem.at[q],
                device_id=(owner, code), device_id_type=MESH,
            ).start()
        pltpu.make_async_copy(sent.at[q, me], received.at[q, PEERS], own_sem.at[q]).start()

    def all_ids():
        return pltpu.make_async_remote_copy(
            src_ref=id_send.at[pl.ds(0, PEERS)], dst_ref=id_recv.at[pl.ds(0, PEERS)],
            send_sem=id_send_sem, recv_sem=id_recv_sem, device_id=(me, code), device_id_type=MESH,
        )

    def whole_chunk(q):
        return pltpu.make_async_remote_copy(
            src_ref=sent.at[q, pl.ds(0, PEERS)], dst_ref=received.at[q, pl.ds(0, PEERS)],
            send_sem=send_sem.at[q], recv_sem=recv_sem.at[q], device_id=(me, code), device_id_type=MESH,
        )

    def build_selector():
        all_ids().wait_recv()
        ids = jnp.concatenate([id_recv[i] for i in range(PEERS)] + [id_send[me]], axis=0)
        row_in_chunk = lax.broadcasted_iota(jnp.int32, (OWNERS, E), 1) % ROWS
        keys = jnp.full((OWNERS, E), -1, jnp.int32)
        for b in range(BLOCKS):
            keys = jnp.where(ids == b, slot_ref[0, b] * ROWS + row_in_chunk, keys)
        pairs = []
        for i in range(PAIRS):
            low, high = keys[2 * i : 2 * i + 1, :], keys[2 * i + 1 : 2 * i + 2, :]
            pairs.append(jnp.broadcast_to(jnp.where(lane < SLOT_ROWS, low, high), (ROWS, E)))
        row_index = lax.broadcasted_iota(jnp.int32, (ROWS, E), 0)

        def selector_rows(p, carry):
            wanted = row_index + p * ROWS
            tiles = [jnp.where(pair == wanted, 1.0, 0.0).astype(jnp.bfloat16) for pair in pairs]
            selector[pl.ds(pl.multiple_of(p * ROWS, ROWS), ROWS), :] = jnp.concatenate(tiles, axis=1)
            return carry

        lax.fori_loop(0, BLOCKS, selector_rows, 0)

    def delta_copies(q):
        copies = []
        for step in range(1, CODERS):
            holder = (code + step) % CODERS
            copies.append(
                pltpu.make_async_remote_copy(
                    src_ref=delta_send.at[q, pl.ds(holder * HELD, HELD)], dst_ref=delta_recv.at[q, step - 1],
                    send_sem=delta_send_sem.at[q], recv_sem=delta_recv_sem.at[q],
                    device_id=(me, holder), device_id_type=MESH,
                )
            )
        return copies

    def all_deltas(q):
        span = pl.ds(0, (CODERS - 1) * HELD)
        return pltpu.make_async_remote_copy(
            src_ref=delta_send.at[q, span], dst_ref=delta_send.at[q, span],
            send_sem=delta_send_sem.at[q], recv_sem=delta_recv_sem.at[q], device_id=(me, code), device_id_type=MESH,
        )

    def table_copy(q):
        rows = pl.ds(pl.multiple_of(q * ROWS, ROWS), ROWS)
        return pltpu.make_async_copy(table.at[:, rows, :], table_out.at[:, rows, :], table_sem.at[q])

    def parity_copy(q):
        rows = pl.ds(pl.multiple_of(q * ROWS, ROWS), ROWS)
        return pltpu.make_async_copy(parity.at[:, rows, :], parity_out.at[:, rows, :], parity_sem.at[q])

    def combine(q):
        rows = pl.ds(pl.multiple_of(q * ROWS, ROWS), ROWS)
        whole_chunk(q).wait_recv()
        pltpu.make_async_copy(sent.at[q, me], received.at[q, PEERS], own_sem.at[q]).wait()
        terms = received[q].reshape(OWNERS * SLOT_ROWS, E)
        old = accum_t[rows, :]

        def block_group(m, carry):
            first = pl.multiple_of(m * (PARITY_GROUP * ROWS), PARITY_GROUP * ROWS)
            sums = jnp.dot(selector[pl.ds(first, PARITY_GROUP * ROWS), :], terms, preferred_element_type=jnp.float32)
            grad = sums.astype(jnp.bfloat16).astype(jnp.float32).reshape(PARITY_GROUP, ROWS, E)
            block = lax.broadcasted_iota(jnp.int32, (PARITY_GROUP, ROWS, E), 0) + m * PARITY_GROUP
            mine = slot_lanes.reshape(1, 1, E) == block
            accum = jnp.sum(jnp.where(mine, old[None], 0.0), axis=-1, keepdims=True)
            accum = accum + jnp.sum(grad * grad, axis=-1, keepdims=True) * (1.0 / E)
            change = grad * (-LEARN_RATE * lax.rsqrt(accum))
            delta[pl.ds(m * PARITY_GROUP, PARITY_GROUP)] = change
            delta_send[q, pl.ds(m * PARITY_GROUP, PARITY_GROUP)] = change.astype(jnp.bfloat16)
            new_accum_t[rows, :] += jnp.sum(jnp.where(mine, accum, 0.0), axis=0)
            return carry

        lax.fori_loop(0, BLOCKS // PARITY_GROUP, block_group, 0)
        for copy in delta_copies(q):
            copy.start()

        def add_block(i, carry):
            for j in range(8):
                b = i * 8 + j
                table[b, rows, :] += delta[slot_ref[0, b]]
            return carry

        lax.fori_loop(0, BLOCKS // 8, add_block, 0)
        table_copy(q).start()
        parity[:, rows, :] += delta[pl.ds(code * HELD, HELD)]

    def finish(q):
        rows = pl.ds(pl.multiple_of(q * ROWS, ROWS), ROWS)
        all_deltas(q).wait_recv()
        total = parity[:, rows, :]
        for j in range(CODERS - 1):
            total += delta_recv[q, j].astype(jnp.float32)
        parity[:, rows, :] = total
        parity_copy(q).start()

    def step(s, carry):
        @pl.when(s < CHUNKS)
        def _():
            slot_terms(s)

        @pl.when(s == 0)
        def _():
            pl.semaphore_wait(barrier, PEERS + CODERS - 1)
            send_ids()

        @pl.when(s < CHUNKS)
        def _():
            send_chunk(s)

        @pl.when(s == 1)
        def _():
            build_selector()

        @pl.when(s == LAG)
        def _():
            loads[2].wait()
            loads[3].wait()

        @pl.when((s >= LAG) & (s < CHUNKS + LAG))
        def _():
            combine(s - LAG)

        @pl.when(s >= LAG + 2)
        def _():
            finish(s - LAG - 2)

        return carry

    lax.fori_loop(0, CHUNKS + LAG + 2, step, 0)
    accum_out[...] = new_accum_t[...].T[:BLOCKS, :]

    all_ids().wait_send()

    def drain(q, carry):
        whole_chunk(q).wait_send()
        all_deltas(q).wait_send()
        table_copy(q).wait()
        parity_copy(q).wait()
        return carry

    lax.fori_loop(0, CHUNKS, drain, 0)


def body(pooled_grad, bag_rows, dest_blocks, block_counts, table, accum, parity, parity_slot):
    anywhere = pl.BlockSpec(memory_space=pl.ANY)
    vmem = pl.BlockSpec(memory_space=pltpu.VMEM)
    smem = pl.BlockSpec(memory_space=pltpu.SMEM)
    dma = pltpu.SemaphoreType.DMA
    f32, bf16, i32 = jnp.float32, jnp.bfloat16, jnp.int32
    new_table, new_accum, new_parity = pl.pallas_call(
        kernel,
        name="adagrad_step",
        out_shape=(
            jax.ShapeDtypeStruct((BLOCKS, BLK, E), f32),
            jax.ShapeDtypeStruct((BLOCKS, BLK), f32),
            jax.ShapeDtypeStruct((HELD, BLK, E), f32),
        ),
        in_specs=[anywhere, anywhere, smem, smem, anywhere, vmem, anywhere, smem],
        out_specs=(anywhere, vmem, anywhere),
        scratch_shapes=[
            pltpu.VMEM((BATCH, E), bf16),
            pltpu.VMEM((OWNERS, CAP, BATCH), i32),
            pltpu.VMEM((OWNERS, 1, E), i32),
            pltpu.VMEM((PEERS, 1, E), i32),
            pltpu.VMEM((CHUNKS, OWNERS, SLOT_ROWS, E), bf16),
            pltpu.VMEM((CHUNKS, OWNERS, SLOT_ROWS, E), bf16),
            pltpu.VMEM((BLOCKS * ROWS, OWNERS * SLOT_ROWS), bf16),
            pltpu.VMEM((BLOCKS, BLK, E), f32),
            pltpu.VMEM((HELD, BLK, E), f32),
            pltpu.VMEM((BLK, BLK), f32),
            pltpu.VMEM((BLK, BLK), f32),
            pltpu.VMEM((BLOCKS, ROWS, E), f32),
            pltpu.VMEM((CHUNKS, BLOCKS, ROWS, E), bf16),
            pltpu.VMEM((CHUNKS, CODERS - 1, HELD, ROWS, E), bf16),
            dma((4,)),
            dma,
            dma,
            dma((CHUNKS,)),
            dma((CHUNKS,)),
            dma((CHUNKS,)),
            dma((CHUNKS,)),
            dma((CHUNKS,)),
            dma((CHUNKS,)),
            dma((CHUNKS,)),
        ],
        compiler_params=pltpu.CompilerParams(
            collective_id=0, has_side_effects=True, vmem_limit_bytes=56 * 1024 * 1024
        ),
    )(
        pooled_grad[0, 0], bag_rows[0, 0], dest_blocks[0, 0].T, block_counts[0],
        table[0, 0], accum[0, 0], parity[0], parity_slot[0],
    )
    return (new_table[None, None], new_accum[None, None], new_parity[None])


def solution(mesh):
    placed = (
        P("table", "code", None, None),
        P("table", "code", None, None, None),
        P("table", "code", None, None),
        P("table", "code", None),
        P("table", "code", None, None, None),
        P("table", "code", None, None),
        P("table", "code", None, None),
        P("table", "code", None),
    )
    return jax.shard_map(
        body,
        mesh=mesh,
        in_specs=placed,
        out_specs=(
            P("table", "code", None, None, None),
            P("table", "code", None, None),
            P("table", "code", None, None),
        ),
        check_vma=False,
    )
```

```python
import jax
import jax.numpy as jnp
from jax import lax
from jax.experimental import pallas as pl
from jax.experimental.pallas import tpu as pltpu
from jax.sharding import PartitionSpec as P

LEARN_RATE = 0.2
MESH = pl.DeviceIdType.MESH

RING = 4
CORES = 2
OWNERS = RING * RING * CORES
CODERS = 4
CAP = 4
E = 128
BLK = 128
BLOCKS = 96
HELD = BLOCKS // CODERS
BATCH = 2048

UNIT = 8
UNITS = BLK // UNIT
UNIT_TERMS = CAP * UNIT
WIDE_UNITS, WIDE_CHUNKS = 2, 7
THIN_UNITS, THIN_CHUNKS = 1, 2
DOT_ROWS = 512
LAG = 2


def send_order():
    offsets = [(dz, dx, dc) for dz in range(RING) for dx in range(RING) for dc in range(CORES)][1:]
    offsets.sort(key=lambda m: -(min(m[0], RING - m[0]) + min(m[1], RING - m[1])))
    order = []
    for dz, dx, dc in offsets:
        for _ in range(4):
            if (dz, dx, dc) not in order:
                order.append((dz, dx, dc))
            dz, dx = dx, (RING - dz) % RING
    return order


ORDER = send_order()
PEERS = len(ORDER)


class Stage:
    def __init__(self, units, first_unit, first_chunk, chunks, env, scratch):
        self.units, self.first_unit, self.first_chunk, self.chunks = units, first_unit, first_chunk, chunks
        self.env = env
        self.sent, self.received, self.send_sem, self.recv_sem = scratch

    @staticmethod
    def scratch_shapes(units, chunks):
        bf16, dma = jnp.bfloat16, pltpu.SemaphoreType.DMA
        return [
            pltpu.VMEM((chunks, PEERS, units * UNIT_TERMS, E), bf16),
            pltpu.VMEM((chunks, OWNERS, units * UNIT_TERMS, E), bf16),
            dma((chunks,)),
            dma((chunks,)),
        ]

    def send_terms(self, q, before_first_send=None):
        env = self.env
        terms = self.units * UNIT_TERMS
        row_index = lax.broadcasted_iota(jnp.int32, (UNIT, E), 0) + (self.first_unit + q * self.units) * UNIT
        group = DOT_ROWS // terms
        for start in range(0, OWNERS, group):
            tiles, part = [], []
            for i in range(start, start + group):
                owner = env.owners[i]
                for h in range(self.units):
                    for k in range(CAP):
                        wanted = jnp.where(k < env.counts[0, owner], row_index + h * UNIT, -1)
                        wanted = jnp.concatenate([wanted] * (BATCH // E), axis=1)
                        part.append(jnp.where(env.bags[owner, pl.ds(k, 1), :] == wanted, 1.0, 0.0))
                        if len(part) == 2:
                            tiles.append(jnp.concatenate(part, axis=0).astype(jnp.bfloat16))
                            part = []
            onehot = jnp.concatenate(tiles, axis=0)
            sums = jnp.dot(onehot, env.pooled[...], preferred_element_type=jnp.float32)
            sums = sums.astype(jnp.bfloat16).reshape(group, terms, E)
            if start + group < OWNERS:
                self.sent[q, pl.ds(start, group)] = sums
            else:
                self.sent[q, pl.ds(start, group - 1)] = sums[: group - 1]
                self.received[q, PEERS] = sums[group - 1]
        if before_first_send is not None:
            before_first_send()
        for i in range(PEERS):
            pltpu.make_async_remote_copy(
                src_ref=self.sent.at[q, i], dst_ref=self.received.at[q, i],
                send_sem=self.send_sem.at[q], recv_sem=self.recv_sem.at[q],
                device_id=(env.owners[i], env.code), device_id_type=MESH,
            ).start()

    def all_terms(self, q):
        return pltpu.make_async_remote_copy(
            src_ref=self.sent.at[q], dst_ref=self.received.at[q, pl.ds(0, PEERS)],
            send_sem=self.send_sem.at[q], recv_sem=self.recv_sem.at[q],
            device_id=(self.env.me, self.env.code), device_id_type=MESH,
        )

    def combine(self, q):
        env = self.env
        self.all_terms(q).wait_recv()

        def combine_unit(h, carry):
            unit = self.first_unit + q * self.units + h
            first = pl.multiple_of(h * UNIT_TERMS, UNIT_TERMS)
            env.combine_unit(unit, h, self.received[q, :, pl.ds(first, UNIT_TERMS), :])
            return carry

        lax.fori_loop(0, self.units, combine_unit, 0)
        rows = self.units * UNIT
        first_row = pl.multiple_of((self.first_unit + q * self.units) * UNIT, UNIT)

        def add_blocks(i, carry):
            for j in range(8):
                b = i * 8 + j
                env.table[b, pl.ds(first_row, rows), :] += env.delta[env.slots[0, b], pl.ds(0, rows), :]
            return carry

        lax.fori_loop(0, BLOCKS // 8, add_blocks, 0)

    def finish(self, q):
        def finish_unit(h, carry):
            self.env.finish_unit(self.first_unit + q * self.units + h)
            return carry

        lax.fori_loop(0, self.units, finish_unit, 0)

    def at(self, s, do):
        @pl.when((s >= self.first_chunk) & (s < self.first_chunk + self.chunks))
        def _():
            do(s - self.first_chunk)

    def drain(self):
        def wait(q, carry):
            self.all_terms(q).wait_send()
            return carry

        lax.fori_loop(0, self.chunks, wait, 0)


class Env:
    def build_selector(self):
        ids = jnp.concatenate([self.id_recv[i] for i in range(PEERS)] + [self.id_send[PEERS]], axis=0)
        row_in_unit = lax.broadcasted_iota(jnp.int32, (OWNERS, E), 1) % UNIT
        keys = jnp.full((OWNERS, E), -1, jnp.int32)
        for b in range(BLOCKS):
            keys = jnp.where(ids == b, self.slots[0, b] * UNIT + row_in_unit, keys)
        lane = lax.broadcasted_iota(jnp.int32, (1, E), 1)
        per_tile = E // UNIT_TERMS
        lane_tiles = []
        for first in range(0, OWNERS, per_tile):
            tile = keys[first : first + 1, :]
            for j in range(1, per_tile):
                tile = jnp.where(lane >= j * UNIT_TERMS, keys[first + j : first + j + 1, :], tile)
            lane_tiles.append(jnp.broadcast_to(tile, (16, E)))
        row_index = lax.broadcasted_iota(jnp.int32, (16, E), 0)

        def selector_rows(p, carry):
            wanted = row_index + p * 16
            tiles = [jnp.where(tile == wanted, 1.0, 0.0).astype(jnp.bfloat16) for tile in lane_tiles]
            self.selector[pl.ds(pl.multiple_of(p * 16, 16), 16), :] = jnp.concatenate(tiles, axis=1)
            return carry

        lax.fori_loop(0, BLOCKS * UNIT // 16, selector_rows, 0)

    def combine_unit(self, unit, h, terms):
        block_rows = pl.ds(pl.multiple_of(unit * UNIT, UNIT), UNIT)
        delta_rows = pl.ds(pl.multiple_of(h * UNIT, UNIT), UNIT)
        terms = terms.reshape(OWNERS * UNIT_TERMS, E)
        sums = jnp.dot(self.selector[...], terms, preferred_element_type=jnp.float32)
        grad = sums.astype(jnp.bfloat16).astype(jnp.float32).reshape(BLOCKS, UNIT, E)
        mine = self.slot_lanes.reshape(1, 1, E) == lax.broadcasted_iota(jnp.int32, (BLOCKS, UNIT, E), 0)
        old = self.accum_t[block_rows, :] * float(E)
        accum = jnp.sum(jnp.where(mine, old[None], 0.0) + grad * grad, axis=-1, keepdims=True) * (1.0 / E)
        change = grad * (-LEARN_RATE * lax.rsqrt(accum))
        self.delta_send[unit] = change.astype(jnp.bfloat16).reshape(BLOCKS * UNIT, E)
        for step in range(1, CODERS):
            holder = (self.code + step) % CODERS
            span = pl.ds(pl.multiple_of(holder * (HELD * UNIT), HELD * UNIT), HELD * UNIT)
            pltpu.make_async_remote_copy(
                src_ref=self.delta_send.at[unit, span], dst_ref=self.delta_recv.at[unit, step - 1],
                send_sem=self.delta_send_sem.at[unit], recv_sem=self.delta_recv_sem.at[unit],
                device_id=(self.me, holder), device_id_type=MESH,
            ).start()
        self.delta[:, delta_rows, :] = change
        self.new_accum_t[block_rows, :] = jnp.sum(jnp.where(mine, accum, 0.0), axis=0)
        self.parity[:, block_rows, :] += self.delta[pl.ds(self.code * HELD, HELD), delta_rows, :]

    def all_deltas(self, unit):
        return pltpu.make_async_remote_copy(
            src_ref=self.delta_recv.at[unit], dst_ref=self.delta_recv.at[unit],
            send_sem=self.delta_send_sem.at[unit], recv_sem=self.delta_recv_sem.at[unit],
            device_id=(self.me, self.code), device_id_type=MESH,
        )

    def finish_unit(self, unit):
        block_rows = pl.ds(pl.multiple_of(unit * UNIT, UNIT), UNIT)
        self.all_deltas(unit).wait_recv()
        total = self.parity[:, block_rows, :]
        for j in range(CODERS - 1):
            total += self.delta_recv[unit, j].astype(jnp.float32).reshape(HELD, UNIT, E)
        self.parity[:, block_rows, :] = total

    def drain(self):
        def wait(unit, carry):
            self.all_deltas(unit).wait_send()
            return carry

        lax.fori_loop(0, UNITS, wait, 0)


def kernel(
    pooled_hbm, bags_hbm, dest_hbm, counts_hbm, table_hbm, accum_hbm, parity_hbm, slots_hbm,
    table, accum_out, parity,
    pooled, bags, dest, counts, slots, accum, id_send, id_recv, accum_t, new_accum_t,
    selector, delta, delta_send, delta_recv,
    in_sem, id_send_sem, id_recv_sem, delta_send_sem, delta_recv_sem, *stage_scratch,
):
    me = lax.axis_index("table")
    code = lax.axis_index("code")
    z, x, core = me // (RING * CORES), (me // CORES) % RING, me % CORES
    owners = [
        (((z + dz) % RING) * RING + (x + dx) % RING) * CORES + (core + dc) % CORES for dz, dx, dc in ORDER
    ] + [me]

    env = Env()
    env.me, env.code, env.owners = me, code, owners
    env.pooled, env.bags, env.counts, env.slots = pooled, bags, counts, slots
    env.id_send, env.id_recv, env.accum_t, env.new_accum_t = id_send, id_recv, accum_t, new_accum_t
    env.selector, env.delta, env.delta_send, env.delta_recv = selector, delta, delta_send, delta_recv
    env.delta_send_sem, env.delta_recv_sem = delta_send_sem, delta_recv_sem
    env.table, env.parity = table, parity
    half = len(stage_scratch) // 2
    wide = Stage(WIDE_UNITS, 0, 0, WIDE_CHUNKS, env, stage_scratch[:half])
    thin = Stage(THIN_UNITS, WIDE_UNITS * WIDE_CHUNKS, WIDE_CHUNKS, THIN_CHUNKS, env, stage_scratch[half:])
    stages = (wide, thin)

    sources = (counts_hbm, dest_hbm, slots_hbm, pooled_hbm, bags_hbm, accum_hbm, table_hbm, parity_hbm)
    places = (counts, dest, slots, pooled, bags, accum, table, parity)
    loads = [pltpu.make_async_copy(a, b, in_sem.at[i]) for i, (a, b) in enumerate(zip(sources, places))]
    for load in loads[:6]:
        load.start()

    barrier = pltpu.get_barrier_semaphore()
    for owner in owners[:PEERS]:
        pl.semaphore_signal(barrier, inc=1, device_id=(owner, code), device_id_type=MESH)
    for step in range(1, CODERS):
        pl.semaphore_signal(barrier, inc=1, device_id=(me, (code + step) % CODERS), device_id_type=MESH)

    for load in loads[:5]:
        load.wait()

    def send_ids():
        lane_slot = (lax.broadcasted_iota(jnp.int32, (1, E), 1) // UNIT) % CAP
        for i, owner in enumerate(owners):
            ids = jnp.full((1, E), -1, jnp.int32)
            for k in range(CAP):
                ids = jnp.where((lane_slot == k) & (k < counts[0, owner]), dest[k, owner], ids)
            id_send[i] = ids
        for i, owner in enumerate(owners[:PEERS]):
            pltpu.make_async_remote_copy(
                src_ref=id_send.at[i], dst_ref=id_recv.at[i], send_sem=id_send_sem, recv_sem=id_recv_sem,
                device_id=(owner, code), device_id_type=MESH,
            ).start()

    def all_ids():
        return pltpu.make_async_remote_copy(
            src_ref=id_send.at[pl.ds(0, PEERS)], dst_ref=id_recv, send_sem=id_send_sem, recv_sem=id_recv_sem,
            device_id=(me, code), device_id_type=MESH,
        )

    lane = lax.broadcasted_iota(jnp.int32, (1, E), 1)
    env.slot_lanes = jnp.full((1, E), -1, jnp.int32)
    for b in range(BLOCKS):
        env.slot_lanes = jnp.where(lane == b, slots[0, b], env.slot_lanes)

    def step(s, carry):
        def all_here():
            @pl.when(s == 0)
            def _():
                pl.semaphore_wait(barrier, PEERS + CODERS - 1)

        wide.at(s, lambda q: wide.send_terms(q, all_here))
        thin.at(s, thin.send_terms)

        @pl.when(s == 0)
        def _():
            send_ids()
            loads[6].start()
            loads[7].start()
            loads[5].wait()
            padding = jnp.zeros((BLK - BLOCKS, BLK), jnp.float32)
            accum_t[...] = jnp.concatenate([accum[...], padding], axis=0).T

        @pl.when(s == 1)
        def _():
            all_ids().wait_recv()
            env.build_selector()
            loads[6].wait()
            loads[7].wait()

        for stage in stages:
            stage.at(s - LAG, stage.combine)
        for stage in stages:
            stage.at(s - LAG - 2, stage.finish)
        return carry

    lax.fori_loop(0, WIDE_CHUNKS + THIN_CHUNKS + LAG + 2, step, 0)
    accum_out[...] = new_accum_t[...].T[:BLOCKS, :]
    all_ids().wait_send()
    env.drain()
    for stage in stages:
        stage.drain()


def body(pooled_grad, bag_rows, dest_blocks, block_counts, table, accum, parity, parity_slot):
    hbm = pl.BlockSpec(memory_space=pltpu.HBM)
    vmem = pl.BlockSpec(memory_space=pltpu.VMEM)
    dma = pltpu.SemaphoreType.DMA
    f32, bf16, i32 = jnp.float32, jnp.bfloat16, jnp.int32
    results = ((BLOCKS, BLK, E), (BLOCKS, BLK), (HELD, BLK, E))
    arrays = (
        pooled_grad[0, 0], bag_rows[0, 0], dest_blocks[0, 0].T, block_counts[0],
        table[0, 0], accum[0, 0], parity[0], parity_slot[0],
    )
    new_table, new_accum, new_parity = pl.pallas_call(
        kernel,
        name="adagrad_step",
        out_shape=[pltpu.VMEM(shape, f32) for shape in results],
        in_specs=[hbm] * len(arrays),
        out_specs=[vmem] * len(results),
        scratch_shapes=[
            pltpu.VMEM((BATCH, E), bf16),
            pltpu.VMEM((OWNERS, CAP, BATCH), i32),
            pltpu.SMEM((CAP, OWNERS), i32),
            pltpu.SMEM((1, OWNERS), i32),
            pltpu.SMEM((1, BLOCKS), i32),
            pltpu.VMEM((BLOCKS, BLK), f32),
            pltpu.VMEM((OWNERS, 1, E), i32),
            pltpu.VMEM((PEERS, 1, E), i32),
            pltpu.VMEM((BLK, BLK), f32),
            pltpu.VMEM((BLK, BLK), f32),
            pltpu.VMEM((BLOCKS * UNIT, OWNERS * UNIT_TERMS), bf16),
            pltpu.VMEM((BLOCKS, WIDE_UNITS * UNIT, E), f32),
            pltpu.VMEM((UNITS, BLOCKS * UNIT, E), bf16),
            pltpu.VMEM((UNITS, CODERS - 1, HELD * UNIT, E), bf16),
            dma((len(arrays),)),
            dma,
            dma,
            dma((UNITS,)),
            dma((UNITS,)),
            *Stage.scratch_shapes(WIDE_UNITS, WIDE_CHUNKS),
            *Stage.scratch_shapes(THIN_UNITS, THIN_CHUNKS),
        ],
        compiler_params=pltpu.CompilerParams(
            collective_id=0, has_side_effects=True, vmem_limit_bytes=40 * 1024 * 1024
        ),
    )(*[pltpu.with_memory_space_constraint(array, pltpu.HBM) for array in arrays])
    return (new_table[None, None], new_accum[None, None], new_parity[None])


def solution(mesh):
    placed = (
        P("table", "code", None, None),
        P("table", "code", None, None, None),
        P("table", "code", None, None),
        P("table", "code", None),
        P("table", "code", None, None, None),
        P("table", "code", None, None),
        P("table", "code", None, None),
        P("table", "code", None),
    )
    return jax.shard_map(
        body,
        mesh=mesh,
        in_specs=placed,
        out_specs=(
            P("table", "code", None, None, None),
            P("table", "code", None, None),
            P("table", "code", None, None),
        ),
        check_vma=False,
    )
```

```python
import jax
import jax.numpy as jnp
from jax import lax
from jax.experimental import pallas as pl
from jax.experimental.pallas import tpu as pltpu
from jax.sharding import PartitionSpec as P

LEARN_RATE = 0.2
MESH = pl.DeviceIdType.MESH

RING = 4
CORES = 2
OWNERS = RING * RING * CORES
CODERS = 4
CAP = 4
E = 128
BLK = 128
BLOCKS = 96
HELD = BLOCKS // CODERS
BATCH = 2048

UNIT = 8
UNITS = BLK // UNIT
UNIT_TERMS = CAP * UNIT
WIDE_UNITS, WIDE_CHUNKS = 2, 7
THIN_UNITS, THIN_CHUNKS = 1, 2
CHUNKS = WIDE_CHUNKS + THIN_CHUNKS
DOT_ROWS = 512
LAG = 2


def send_order():
    offsets = [(dz, dx, dc) for dz in range(RING) for dx in range(RING) for dc in range(CORES)][1:]
    offsets.sort(key=lambda m: -(min(m[0], RING - m[0]) + min(m[1], RING - m[1])))
    order = []
    for dz, dx, dc in offsets:
        for _ in range(4):
            if (dz, dx, dc) not in order:
                order.append((dz, dx, dc))
            dz, dx = dx, (RING - dz) % RING
    return order


ORDER = send_order()
BAG_PARTS = [pl.ds(0, OWNERS // 2), pl.ds(OWNERS // 2, OWNERS // 2)]
PEERS = len(ORDER)


class Stage:
    def __init__(self, units, chunks, unit_of, half_of, env, scratch):
        self.units, self.chunks, self.unit_of, self.half_of = units, chunks, unit_of, half_of
        self.env = env
        self.sent, self.received, self.send_sem, self.recv_sem = scratch

    @staticmethod
    def scratch_shapes(units, chunks):
        bf16, dma = jnp.bfloat16, pltpu.SemaphoreType.DMA
        return [
            pltpu.VMEM((chunks, PEERS, units * UNIT_TERMS, E), bf16),
            pltpu.VMEM((chunks, OWNERS, units * UNIT_TERMS, E), bf16),
            dma((chunks,)),
            dma((chunks,)),
        ]

    def send_terms(self, q, before_first_send=None):
        env = self.env
        terms = self.units * UNIT_TERMS
        row_index = lax.broadcasted_iota(jnp.int32, (UNIT, E), 0) + self.unit_of(q) * UNIT
        group = DOT_ROWS // terms
        for start in range(0, OWNERS, group):
            tiles, part = [], []
            for i in range(start, start + group):
                owner = env.owners[i]
                for h in range(self.units):
                    for k in range(CAP):
                        wanted = jnp.where(k < env.counts[0, owner], row_index + h * UNIT, -1)
                        wanted = jnp.concatenate([wanted] * (BATCH // E), axis=1)
                        part.append(jnp.where(env.bags[owner, pl.ds(k, 1), :] == wanted, 1.0, 0.0))
                        if len(part) == 2:
                            tiles.append(jnp.concatenate(part, axis=0).astype(jnp.bfloat16))
                            part = []
            onehot = jnp.concatenate(tiles, axis=0)
            sums = jnp.dot(onehot, env.pooled[...], preferred_element_type=jnp.float32)
            sums = sums.astype(jnp.bfloat16).reshape(group, terms, E)
            if start + group < OWNERS:
                self.sent[q, pl.ds(start, group)] = sums
            else:
                self.sent[q, pl.ds(start, group - 1)] = sums[: group - 1]
                self.received[q, PEERS] = sums[group - 1]
            if self.units == THIN_UNITS:
                self.send(q, start, start + group, before_first_send if start == 0 else None)
        if self.units != THIN_UNITS:
            self.send(q, 0, OWNERS, before_first_send)

    def send(self, q, first, last, before):
        env = self.env
        if before is not None:
            before()
        for i in range(first, min(last, PEERS)):
            pltpu.make_async_remote_copy(
                src_ref=self.sent.at[q, i], dst_ref=self.received.at[q, i],
                send_sem=self.send_sem.at[q], recv_sem=self.recv_sem.at[q],
                device_id=(env.owners[i], env.code), device_id_type=MESH,
            ).start()

    def all_terms(self, q):
        return pltpu.make_async_remote_copy(
            src_ref=self.sent.at[q], dst_ref=self.received.at[q, pl.ds(0, PEERS)],
            send_sem=self.send_sem.at[q], recv_sem=self.recv_sem.at[q],
            device_id=(self.env.me, self.env.code), device_id_type=MESH,
        )

    def combine(self, q):
        env = self.env
        self.all_terms(q).wait_recv()

        def combine_unit(h, carry):
            unit = self.unit_of(q) + h
            first = pl.multiple_of(h * UNIT_TERMS, UNIT_TERMS)
            env.combine_unit(unit, self.half_of(q), h, self.received[q, :, pl.ds(first, UNIT_TERMS), :])
            return carry

        lax.fori_loop(0, self.units, combine_unit, 0)

    def add_blocks(self, q):
        env = self.env
        half = self.half_of(q)
        rows = self.units * UNIT
        first_row = pl.multiple_of(self.unit_of(q) * UNIT, UNIT)

        def add_some(i, carry):
            for j in range(8):
                b = i * 8 + j
                env.table[b, pl.ds(first_row, rows), :] += env.delta[half, env.slots[0, b], pl.ds(0, rows), :]
            return carry

        lax.fori_loop(0, BLOCKS // 8, add_some, 0)

    def finish(self, q):
        def finish_unit(h, carry):
            self.env.finish_unit(self.unit_of(q) + h)
            return carry

        lax.fori_loop(0, self.units, finish_unit, 0)

    def drain(self):
        def wait(q, carry):
            self.all_terms(q).wait_send()
            return carry

        lax.fori_loop(0, self.chunks, wait, 0)


class Env:
    def build_selector(self):
        ids = jnp.concatenate([self.id_recv[i] for i in range(PEERS)] + [self.id_send[PEERS]], axis=0)
        row_in_unit = lax.broadcasted_iota(jnp.int32, (OWNERS, E), 1) % UNIT
        keys = jnp.full((OWNERS, E), -1, jnp.int32)
        for b in range(BLOCKS):
            keys = jnp.where(ids == b, self.slots[0, b] * UNIT + row_in_unit, keys)
        lane = lax.broadcasted_iota(jnp.int32, (1, E), 1)
        per_tile = E // UNIT_TERMS
        lane_tiles = []
        for first in range(0, OWNERS, per_tile):
            tile = keys[first : first + 1, :]
            for j in range(1, per_tile):
                tile = jnp.where(lane >= j * UNIT_TERMS, keys[first + j : first + j + 1, :], tile)
            lane_tiles.append(jnp.broadcast_to(tile, (16, E)))
        row_index = lax.broadcasted_iota(jnp.int32, (16, E), 0)

        def selector_rows(p, carry):
            wanted = row_index + p * 16
            tiles = [jnp.where(tile == wanted, 1.0, 0.0).astype(jnp.bfloat16) for tile in lane_tiles]
            self.selector[pl.ds(pl.multiple_of(p * 16, 16), 16), :] = jnp.concatenate(tiles, axis=1)
            return carry

        lax.fori_loop(0, BLOCKS * UNIT // 16, selector_rows, 0)

    def combine_unit(self, unit, half, h, terms):
        block_rows = pl.ds(pl.multiple_of(unit * UNIT, UNIT), UNIT)
        delta_rows = pl.ds(pl.multiple_of(h * UNIT, UNIT), UNIT)
        terms = terms.reshape(OWNERS * UNIT_TERMS, E)
        sums = jnp.dot(self.selector[...], terms, preferred_element_type=jnp.float32)
        grad = sums.astype(jnp.bfloat16).astype(jnp.float32).reshape(BLOCKS, UNIT, E)
        mine = self.slot_lanes[...].reshape(1, 1, E) == lax.broadcasted_iota(jnp.int32, (BLOCKS, UNIT, E), 0)
        old = self.accum_t[block_rows, :] * float(E)
        accum = jnp.sum(jnp.where(mine, old[None], 0.0) + grad * grad, axis=-1, keepdims=True) * (1.0 / E)
        change = grad * (-LEARN_RATE * lax.rsqrt(accum))
        self.delta_send[unit] = change.astype(jnp.bfloat16).reshape(BLOCKS * UNIT, E)
        for step in range(1, CODERS):
            holder = (self.code + step) % CODERS
            span = pl.ds(pl.multiple_of(holder * (HELD * UNIT), HELD * UNIT), HELD * UNIT)
            pltpu.make_async_remote_copy(
                src_ref=self.delta_send.at[unit, span], dst_ref=self.delta_recv.at[unit, step - 1],
                send_sem=self.delta_send_sem.at[unit], recv_sem=self.delta_recv_sem.at[unit],
                device_id=(self.me, holder), device_id_type=MESH,
            ).start()
        self.delta[half, :, delta_rows, :] = change
        self.new_accum_t[block_rows, :] = jnp.sum(jnp.where(mine, accum, 0.0), axis=0)
        self.parity[:, block_rows, :] += self.delta[half, pl.ds(self.code * HELD, HELD), delta_rows, :]

    def all_deltas(self, unit):
        return pltpu.make_async_remote_copy(
            src_ref=self.delta_recv.at[unit], dst_ref=self.delta_recv.at[unit],
            send_sem=self.delta_send_sem.at[unit], recv_sem=self.delta_recv_sem.at[unit],
            device_id=(self.me, self.code), device_id_type=MESH,
        )

    def finish_unit(self, unit):
        block_rows = pl.ds(pl.multiple_of(unit * UNIT, UNIT), UNIT)
        self.all_deltas(unit).wait_recv()
        total = self.parity[:, block_rows, :]
        for j in range(CODERS - 1):
            total += self.delta_recv[unit, j].astype(jnp.float32).reshape(HELD, UNIT, E)
        self.parity[:, block_rows, :] = total

    def drain(self):
        def wait(unit, carry):
            self.all_deltas(unit).wait_send()
            return carry

        lax.fori_loop(0, UNITS, wait, 0)


def kernel(
    pooled_hbm, bags_hbm, dest_hbm, counts_hbm, table_hbm, accum_hbm, parity_hbm, slots_hbm,
    table, accum_out, parity,
    pooled, bags, dest, counts, slots, accum, id_send, id_recv, accum_t, new_accum_t, slot_lanes,
    selector, delta, delta_send, delta_recv,
    in_sem, id_send_sem, id_recv_sem, delta_send_sem, delta_recv_sem, *stage_scratch,
):
    sources = (counts_hbm, pooled_hbm, *[bags_hbm.at[part] for part in BAG_PARTS], dest_hbm, slots_hbm, accum_hbm, table_hbm, parity_hbm)
    places = (counts, pooled, *[bags.at[part] for part in BAG_PARTS], dest, slots, accum, table, parity)
    loads = [pltpu.make_async_copy(a, b, in_sem.at[i]) for i, (a, b) in enumerate(zip(sources, places))]
    first, second, last = loads[:-5], loads[-5:-2], loads[-2:]
    for load in first + second:
        load.start()

    me = lax.axis_index("table")
    code = lax.axis_index("code")
    z, x, core = lax.div(me, RING * CORES), lax.rem(lax.div(me, CORES), RING), lax.rem(me, CORES)
    zs = [lax.rem(z + d, RING) * (RING * CORES) for d in range(RING)]
    xs = [lax.rem(x + d, RING) * CORES for d in range(RING)]
    cores = [core, 1 - core]
    owners = [zs[dz] + xs[dx] + cores[dc] for dz, dx, dc in ORDER] + [me]

    env = Env()
    env.me, env.code, env.owners = me, code, owners
    env.pooled, env.bags, env.counts, env.slots = pooled, bags, counts, slots
    env.id_send, env.id_recv, env.accum_t, env.new_accum_t = id_send, id_recv, accum_t, new_accum_t
    env.selector, env.delta, env.delta_send, env.delta_recv = selector, delta, delta_send, delta_recv
    env.delta_send_sem, env.delta_recv_sem = delta_send_sem, delta_recv_sem
    env.table, env.parity, env.slot_lanes = table, parity, slot_lanes
    half = len(stage_scratch) // 2
    wide = Stage(WIDE_UNITS, WIDE_CHUNKS, lambda q: THIN_UNITS + q * WIDE_UNITS, lambda q: lax.rem(q + 1, 2), env, stage_scratch[:half])
    thin = Stage(THIN_UNITS, THIN_CHUNKS, lambda q: q * (UNITS - THIN_UNITS), lambda q: 0, env, stage_scratch[half:])

    def at_chunk(s, do):
        @pl.when((s == 0) | (s == CHUNKS - 1))
        def _():
            do(thin, s // (CHUNKS - 1))

        @pl.when((s > 0) & (s < CHUNKS - 1))
        def _():
            do(wide, s - 1)


    barrier = pltpu.get_barrier_semaphore()
    for owner in owners[:PEERS]:
        pl.semaphore_signal(barrier, inc=1, device_id=(owner, code), device_id_type=MESH)
    for step in range(1, CODERS):
        pl.semaphore_signal(barrier, inc=1, device_id=(me, (code + step) % CODERS), device_id_type=MESH)

    for load in first:
        load.wait()

    def send_ids():
        lane_slot = (lax.broadcasted_iota(jnp.int32, (1, E), 1) // UNIT) % CAP
        for i, owner in enumerate(owners):
            ids = jnp.full((1, E), -1, jnp.int32)
            for k in range(CAP):
                ids = jnp.where((lane_slot == k) & (k < counts[0, owner]), dest[k, owner], ids)
            id_send[i] = ids
        for i, owner in enumerate(owners[:PEERS]):
            pltpu.make_async_remote_copy(
                src_ref=id_send.at[i], dst_ref=id_recv.at[i], send_sem=id_send_sem, recv_sem=id_recv_sem,
                device_id=(owner, code), device_id_type=MESH,
            ).start()

    def all_ids():
        return pltpu.make_async_remote_copy(
            src_ref=id_send.at[pl.ds(0, PEERS)], dst_ref=id_recv, send_sem=id_send_sem, recv_sem=id_recv_sem,
            device_id=(me, code), device_id_type=MESH,
        )

    def step(s, carry):
        def all_here():
            @pl.when(s == 0)
            def _():
                pl.semaphore_wait(barrier, PEERS + CODERS - 1)

        at_chunk(s, lambda stage, q: stage.send_terms(q, all_here if stage is thin else None))

        @pl.when(s == 0)
        def _():
            for load in last:
                load.start()
            for load in second:
                load.wait()
            send_ids()
            lane = lax.broadcasted_iota(jnp.int32, (1, E), 1)
            lanes = jnp.full((1, E), -1, jnp.int32)
            for b in range(BLOCKS):
                lanes = jnp.where(lane == b, slots[0, b], lanes)
            slot_lanes[...] = lanes
            padding = jnp.zeros((BLK - BLOCKS, BLK), jnp.float32)
            accum_t[...] = jnp.concatenate([accum[...], padding], axis=0).T

        @pl.when(s == 1)
        def _():
            all_ids().wait_recv()
            env.build_selector()
            for load in last:
                load.wait()

        at_chunk(s - LAG, lambda stage, q: stage.combine(q))
        at_chunk(s - LAG - 1, lambda stage, q: stage.add_blocks(q))
        at_chunk(s - LAG - 2, lambda stage, q: stage.finish(q))
        return carry

    lax.fori_loop(0, CHUNKS + LAG + 1, step, 0)
    accum_out[...] = new_accum_t[...].T[:BLOCKS, :]
    all_ids().wait_send()
    wide.drain()
    thin.drain()
    thin.finish(THIN_CHUNKS - 1)
    env.drain()


def store(table, accum, parity, table_out, accum_out, parity_out, sem):
    parts = [(table, table_out, pl.ds(first, HELD)) for first in range(0, BLOCKS, HELD)]
    parts += [(parity, parity_out, pl.ds(0, HELD)), (accum, accum_out, pl.ds(0, BLOCKS))]
    copies = [pltpu.make_async_copy(a.at[part], b.at[part], sem.at[i]) for i, (a, b, part) in enumerate(parts)]
    for copy in copies:
        copy.start()
    for copy in copies:
        copy.wait()


def body(pooled_grad, bag_rows, dest_blocks, block_counts, table, accum, parity, parity_slot):
    hbm = pl.BlockSpec(memory_space=pltpu.HBM)
    vmem = pl.BlockSpec(memory_space=pltpu.VMEM)
    dma = pltpu.SemaphoreType.DMA
    f32, bf16, i32 = jnp.float32, jnp.bfloat16, jnp.int32
    results = ((BLOCKS, BLK, E), (BLOCKS, BLK), (HELD, BLK, E))
    arrays = (
        pooled_grad[0, 0], bag_rows[0, 0], dest_blocks[0, 0].T, block_counts[0],
        table[0, 0], accum[0, 0], parity[0], parity_slot[0],
    )
    updated = pl.pallas_call(
        kernel,
        name="adagrad_step",
        out_shape=[pltpu.VMEM(shape, f32) for shape in results],
        in_specs=[hbm] * len(arrays),
        out_specs=[vmem] * len(results),
        scratch_shapes=[
            pltpu.VMEM((BATCH, E), bf16),
            pltpu.VMEM((OWNERS, CAP, BATCH), i32),
            pltpu.SMEM((CAP, OWNERS), i32),
            pltpu.SMEM((1, OWNERS), i32),
            pltpu.SMEM((1, BLOCKS), i32),
            pltpu.VMEM((BLOCKS, BLK), f32),
            pltpu.VMEM((OWNERS, 1, E), i32),
            pltpu.VMEM((PEERS, 1, E), i32),
            pltpu.VMEM((BLK, BLK), f32),
            pltpu.VMEM((BLK, BLK), f32),
            pltpu.VMEM((1, E), i32),
            pltpu.VMEM((BLOCKS * UNIT, OWNERS * UNIT_TERMS), bf16),
            pltpu.VMEM((2, BLOCKS, WIDE_UNITS * UNIT, E), f32),
            pltpu.VMEM((UNITS, BLOCKS * UNIT, E), bf16),
            pltpu.VMEM((UNITS, CODERS - 1, HELD * UNIT, E), bf16),
            dma((len(arrays) - 1 + len(BAG_PARTS),)),
            dma,
            dma,
            dma((UNITS,)),
            dma((UNITS,)),
            *Stage.scratch_shapes(WIDE_UNITS, WIDE_CHUNKS),
            *Stage.scratch_shapes(THIN_UNITS, THIN_CHUNKS),
        ],
        compiler_params=pltpu.CompilerParams(
            collective_id=0, has_side_effects=True, vmem_limit_bytes=40 * 1024 * 1024
        ),
    )(*[pltpu.with_memory_space_constraint(array, pltpu.HBM) for array in arrays])
    new_table, new_accum, new_parity = pl.pallas_call(
        store,
        name="store_results",
        out_shape=[jax.ShapeDtypeStruct(shape, f32) for shape in results],
        in_specs=[vmem] * len(results),
        out_specs=[hbm] * len(results),
        scratch_shapes=[dma((BLOCKS // HELD + 2,))],
        compiler_params=pltpu.CompilerParams(vmem_limit_bytes=4 * 1024 * 1024),
    )(*updated)
    return (new_table[None, None], new_accum[None, None], new_parity[None])


def solution(mesh):
    placed = (
        P("table", "code", None, None),
        P("table", "code", None, None, None),
        P("table", "code", None, None),
        P("table", "code", None),
        P("table", "code", None, None, None),
        P("table", "code", None, None),
        P("table", "code", None, None),
        P("table", "code", None),
    )
    return jax.shard_map(
        body,
        mesh=mesh,
        in_specs=placed,
        out_specs=(
            P("table", "code", None, None, None),
            P("table", "code", None, None),
            P("table", "code", None, None),
        ),
        check_vma=False,
    )
```

```python
import jax
import jax.numpy as jnp
from jax import lax
from jax.experimental import pallas as pl
from jax.experimental.pallas import tpu as pltpu
from jax.sharding import PartitionSpec as P

LEARN_RATE = 0.2
MESH = pl.DeviceIdType.MESH

RING = 4
CORES = 2
OWNERS = RING * RING * CORES
CODERS = 4
CAP = 4
E = 128
BLK = 128
BLOCKS = 96
HELD = BLOCKS // CODERS
BATCH = 2048

UNIT = 8
UNITS = BLK // UNIT
UNIT_TERMS = CAP * UNIT
WIDE_UNITS, WIDE_CHUNKS = 2, 7
THIN_UNITS, THIN_CHUNKS = 1, 2
CHUNKS = WIDE_CHUNKS + THIN_CHUNKS
DOT_ROWS = 512
LAG = 2


def send_order():
    offsets = [(dz, dx, dc) for dz in range(RING) for dx in range(RING) for dc in range(CORES)][1:]
    offsets.sort(key=lambda m: -(min(m[0], RING - m[0]) + min(m[1], RING - m[1])))
    order = []
    for dz, dx, dc in offsets:
        for _ in range(4):
            if (dz, dx, dc) not in order:
                order.append((dz, dx, dc))
            dz, dx = dx, (RING - dz) % RING
    return order


ORDER = send_order()
BAG_PARTS = [pl.ds(0, OWNERS // 2), pl.ds(OWNERS // 2, OWNERS // 2)]
PEERS = len(ORDER)


class Stage:
    def __init__(self, units, chunks, unit_of, half_of, env, scratch):
        self.units, self.chunks, self.unit_of, self.half_of = units, chunks, unit_of, half_of
        self.env = env
        self.sent, self.received, self.send_sem, self.recv_sem = scratch

    @staticmethod
    def scratch_shapes(units, chunks):
        bf16, dma = jnp.bfloat16, pltpu.SemaphoreType.DMA
        return [
            pltpu.VMEM((chunks, PEERS, units * UNIT_TERMS, E), bf16),
            pltpu.VMEM((chunks, OWNERS, units * UNIT_TERMS, E), bf16),
            dma((chunks,)),
            dma((chunks,)),
        ]

    def send_terms(self, q, before_first_send=None):
        env = self.env
        terms = self.units * UNIT_TERMS
        row_index = lax.broadcasted_iota(jnp.int32, (UNIT, E), 0) + self.unit_of(q) * UNIT
        group = DOT_ROWS // terms
        for start in range(0, OWNERS, group):
            tiles, part = [], []
            for i in range(start, start + group):
                owner = env.owners[i]
                for h in range(self.units):
                    for k in range(CAP):
                        wanted = jnp.where(k < env.counts[0, owner], row_index + h * UNIT, -1)
                        wanted = jnp.concatenate([wanted] * (BATCH // E), axis=1)
                        part.append(jnp.where(env.bags[owner, pl.ds(k, 1), :] == wanted, 1.0, 0.0))
                        if len(part) == 2:
                            tiles.append(jnp.concatenate(part, axis=0).astype(jnp.bfloat16))
                            part = []
            onehot = jnp.concatenate(tiles, axis=0)
            sums = jnp.dot(onehot, env.pooled[...], preferred_element_type=jnp.float32)
            sums = sums.astype(jnp.bfloat16).reshape(group, terms, E)
            if start + group < OWNERS:
                self.sent[q, pl.ds(start, group)] = sums
            else:
                self.sent[q, pl.ds(start, group - 1)] = sums[: group - 1]
                self.received[q, PEERS] = sums[group - 1]
            if self.units == THIN_UNITS:
                self.send(q, start, start + group, before_first_send if start == 0 else None)
        if self.units != THIN_UNITS:
            self.send(q, 0, OWNERS, before_first_send)

    def send(self, q, first, last, before):
        env = self.env
        if before is not None:
            before()
        for i in range(first, min(last, PEERS)):
            pltpu.make_async_remote_copy(
                src_ref=self.sent.at[q, i], dst_ref=self.received.at[q, i],
                send_sem=self.send_sem.at[q], recv_sem=self.recv_sem.at[q],
                device_id=(env.owners[i], env.code), device_id_type=MESH,
            ).start()

    def all_terms(self, q):
        return pltpu.make_async_remote_copy(
            src_ref=self.sent.at[q], dst_ref=self.received.at[q, pl.ds(0, PEERS)],
            send_sem=self.send_sem.at[q], recv_sem=self.recv_sem.at[q],
            device_id=(self.env.me, self.env.code), device_id_type=MESH,
        )

    def combine(self, q):
        env = self.env
        self.all_terms(q).wait_recv()

        def combine_unit(h, carry):
            unit = self.unit_of(q) + h
            first = pl.multiple_of(h * UNIT_TERMS, UNIT_TERMS)
            env.combine_unit(unit, self.half_of(q), h, self.received[q, :, pl.ds(first, UNIT_TERMS), :])
            return carry

        lax.fori_loop(0, self.units, combine_unit, 0)

    def add_blocks(self, q):
        env = self.env
        half = self.half_of(q)
        rows = self.units * UNIT
        first_row = pl.multiple_of(self.unit_of(q) * UNIT, UNIT)

        def add_some(i, carry):
            for j in range(8):
                b = i * 8 + j
                env.table[b, pl.ds(first_row, rows), :] += env.delta[half, env.slots[0, b], pl.ds(0, rows), :]
            return carry

        lax.fori_loop(0, BLOCKS // 8, add_some, 0)

    def finish(self, q):
        def finish_unit(h, carry):
            self.env.finish_unit(self.unit_of(q) + h)
            return carry

        lax.fori_loop(0, self.units, finish_unit, 0)

    def drain(self):
        def wait(q, carry):
            self.all_terms(q).wait_send()
            return carry

        lax.fori_loop(0, self.chunks, wait, 0)


class Env:
    def build_selector(self):
        ids = jnp.concatenate([self.id_recv[i] for i in range(PEERS)] + [self.id_send[PEERS]], axis=0)
        row_in_unit = lax.broadcasted_iota(jnp.int32, (OWNERS, E), 1) % UNIT
        keys = jnp.full((OWNERS, E), -1, jnp.int32)
        for b in range(BLOCKS):
            keys = jnp.where(ids == b, self.slots[0, b] * UNIT + row_in_unit, keys)
        lane = lax.broadcasted_iota(jnp.int32, (1, E), 1)
        per_tile = E // UNIT_TERMS
        lane_tiles = []
        for first in range(0, OWNERS, per_tile):
            tile = keys[first : first + 1, :]
            for j in range(1, per_tile):
                tile = jnp.where(lane >= j * UNIT_TERMS, keys[first + j : first + j + 1, :], tile)
            lane_tiles.append(jnp.broadcast_to(tile, (16, E)))
        row_index = lax.broadcasted_iota(jnp.int32, (16, E), 0)

        def selector_rows(p, carry):
            wanted = row_index + p * 16
            tiles = [jnp.where(tile == wanted, 1.0, 0.0).astype(jnp.bfloat16) for tile in lane_tiles]
            self.selector[pl.ds(pl.multiple_of(p * 16, 16), 16), :] = jnp.concatenate(tiles, axis=1)
            return carry

        lax.fori_loop(0, BLOCKS * UNIT // 16, selector_rows, 0)

    def combine_unit(self, unit, half, h, terms):
        block_rows = pl.ds(pl.multiple_of(unit * UNIT, UNIT), UNIT)
        delta_rows = pl.ds(pl.multiple_of(h * UNIT, UNIT), UNIT)
        terms = terms.reshape(OWNERS * UNIT_TERMS, E)
        old = self.accum_t[block_rows, :] * float(E)
        held_rows = HELD * UNIT
        new_accum = jnp.zeros((UNIT, E), jnp.float32)
        for steps in ((2, 1), (3, 0)):
            copies = []
            for step in steps:
                holder = lax.rem(self.code + step, CODERS)
                span = pl.ds(pl.multiple_of(holder * held_rows, held_rows), held_rows)
                sums = jnp.dot(self.selector[span, :], terms, preferred_element_type=jnp.float32)
                grad = sums.astype(jnp.bfloat16).astype(jnp.float32).reshape(HELD, UNIT, E)
                block = lax.broadcasted_iota(jnp.int32, (HELD, UNIT, E), 0) + holder * HELD
                mine = self.slot_lanes[...].reshape(1, 1, E) == block
                accum = jnp.sum(jnp.where(mine, old[None], 0.0) + grad * grad, axis=-1, keepdims=True) * (1.0 / E)
                change = grad * (-LEARN_RATE * lax.rsqrt(accum))
                new_accum += jnp.sum(jnp.where(mine, accum, 0.0), axis=0)
                self.delta[half, pl.ds(holder * HELD, HELD), delta_rows, :] = change
                if step == 0:
                    self.parity[:, block_rows, :] += change
                else:
                    self.delta_send[unit, span, :] = change.astype(jnp.bfloat16).reshape(held_rows, E)
                    copies.append(
                        pltpu.make_async_remote_copy(
                            src_ref=self.delta_send.at[unit, span], dst_ref=self.delta_recv.at[unit, step - 1],
                            send_sem=self.delta_send_sem.at[unit], recv_sem=self.delta_recv_sem.at[unit],
                            device_id=(self.me, holder), device_id_type=MESH,
                        )
                    )
            for copy in copies:
                copy.start()
        self.new_accum_t[block_rows, :] = new_accum

    def all_deltas(self, unit):
        return pltpu.make_async_remote_copy(
            src_ref=self.delta_recv.at[unit], dst_ref=self.delta_recv.at[unit],
            send_sem=self.delta_send_sem.at[unit], recv_sem=self.delta_recv_sem.at[unit],
            device_id=(self.me, self.code), device_id_type=MESH,
        )

    def finish_unit(self, unit):
        block_rows = pl.ds(pl.multiple_of(unit * UNIT, UNIT), UNIT)
        self.all_deltas(unit).wait_recv()
        total = self.parity[:, block_rows, :]
        for j in range(CODERS - 1):
            total += self.delta_recv[unit, j].astype(jnp.float32).reshape(HELD, UNIT, E)
        self.parity[:, block_rows, :] = total

    def drain(self):
        def wait(unit, carry):
            self.all_deltas(unit).wait_send()
            return carry

        lax.fori_loop(0, UNITS - 1, wait, 0)


def kernel(
    pooled_hbm, bags_hbm, dest_hbm, counts_hbm, table_hbm, accum_hbm, parity_hbm, slots_hbm,
    table, accum_out, parity,
    pooled, bags, dest, counts, slots, accum, id_send, id_recv, accum_t, new_accum_t, slot_lanes,
    selector, delta, delta_send, delta_recv,
    in_sem, id_send_sem, id_recv_sem, delta_send_sem, delta_recv_sem, *stage_scratch,
):
    sources = (counts_hbm, pooled_hbm, *[bags_hbm.at[part] for part in BAG_PARTS], dest_hbm, slots_hbm, accum_hbm, table_hbm, parity_hbm)
    places = (counts, pooled, *[bags.at[part] for part in BAG_PARTS], dest, slots, accum, table, parity)
    loads = [pltpu.make_async_copy(a, b, in_sem.at[i]) for i, (a, b) in enumerate(zip(sources, places))]
    first, second, last = loads[:-5], loads[-5:-2], loads[-2:]
    for load in first + second:
        load.start()

    me = lax.axis_index("table")
    code = lax.axis_index("code")
    z, x, core = lax.div(me, RING * CORES), lax.rem(lax.div(me, CORES), RING), lax.rem(me, CORES)
    zs = [lax.rem(z + d, RING) * (RING * CORES) for d in range(RING)]
    xs = [lax.rem(x + d, RING) * CORES for d in range(RING)]
    cores = [core, 1 - core]
    owners = [zs[dz] + xs[dx] + cores[dc] for dz, dx, dc in ORDER] + [me]

    env = Env()
    env.me, env.code, env.owners = me, code, owners
    env.pooled, env.bags, env.counts, env.slots = pooled, bags, counts, slots
    env.id_send, env.id_recv, env.accum_t, env.new_accum_t = id_send, id_recv, accum_t, new_accum_t
    env.selector, env.delta, env.delta_send, env.delta_recv = selector, delta, delta_send, delta_recv
    env.delta_send_sem, env.delta_recv_sem = delta_send_sem, delta_recv_sem
    env.table, env.parity, env.slot_lanes = table, parity, slot_lanes
    half = len(stage_scratch) // 2
    wide = Stage(WIDE_UNITS, WIDE_CHUNKS, lambda q: THIN_UNITS + q * WIDE_UNITS, lambda q: lax.rem(q + 1, 2), env, stage_scratch[:half])
    thin = Stage(THIN_UNITS, THIN_CHUNKS, lambda q: q * (UNITS - THIN_UNITS), lambda q: 0, env, stage_scratch[half:])

    def at_chunk(s, do):
        @pl.when((s == 0) | (s == CHUNKS - 1))
        def _():
            do(thin, s // (CHUNKS - 1))

        @pl.when((s > 0) & (s < CHUNKS - 1))
        def _():
            do(wide, s - 1)


    barrier = pltpu.get_barrier_semaphore()
    for owner in owners[:PEERS]:
        pl.semaphore_signal(barrier, inc=1, device_id=(owner, code), device_id_type=MESH)
    for step in range(1, CODERS):
        pl.semaphore_signal(barrier, inc=1, device_id=(me, (code + step) % CODERS), device_id_type=MESH)

    for load in first:
        load.wait()

    def send_ids():
        lane_slot = (lax.broadcasted_iota(jnp.int32, (1, E), 1) // UNIT) % CAP
        for i, owner in enumerate(owners):
            ids = jnp.full((1, E), -1, jnp.int32)
            for k in range(CAP):
                ids = jnp.where((lane_slot == k) & (k < counts[0, owner]), dest[k, owner], ids)
            id_send[i] = ids
        for i, owner in enumerate(owners[:PEERS]):
            pltpu.make_async_remote_copy(
                src_ref=id_send.at[i], dst_ref=id_recv.at[i], send_sem=id_send_sem, recv_sem=id_recv_sem,
                device_id=(owner, code), device_id_type=MESH,
            ).start()

    def all_ids():
        return pltpu.make_async_remote_copy(
            src_ref=id_send.at[pl.ds(0, PEERS)], dst_ref=id_recv, send_sem=id_send_sem, recv_sem=id_recv_sem,
            device_id=(me, code), device_id_type=MESH,
        )

    def step(s, carry):
        def all_here():
            @pl.when(s == 0)
            def _():
                pl.semaphore_wait(barrier, PEERS + CODERS - 1)

        at_chunk(s, lambda stage, q: stage.send_terms(q, all_here if stage is thin else None))

        @pl.when(s == 0)
        def _():
            for load in last:
                load.start()
            for load in second:
                load.wait()
            send_ids()
            lane = lax.broadcasted_iota(jnp.int32, (1, E), 1)
            lanes = jnp.full((1, E), -1, jnp.int32)
            for b in range(BLOCKS):
                lanes = jnp.where(lane == b, slots[0, b], lanes)
            slot_lanes[...] = lanes
            padding = jnp.zeros((BLK - BLOCKS, BLK), jnp.float32)
            accum_t[...] = jnp.concatenate([accum[...], padding], axis=0).T

        @pl.when(s == 1)
        def _():
            all_ids().wait_recv()
            env.build_selector()
            for load in last:
                load.wait()

        at_chunk(s - LAG, lambda stage, q: stage.combine(q))
        at_chunk(s - LAG - 1, lambda stage, q: stage.add_blocks(q))
        at_chunk(s - LAG - 2, lambda stage, q: stage.finish(q))
        return carry

    lax.fori_loop(0, CHUNKS + LAG + 1, step, 0)
    accum_out[...] = new_accum_t[...].T[:BLOCKS, :]
    all_ids().wait_send()
    wide.drain()
    thin.drain()
    env.drain()
    thin.finish(THIN_CHUNKS - 1)
    env.all_deltas(UNITS - 1).wait_send()


def store(table, accum, parity, table_out, accum_out, parity_out, sem):
    parts = [(table, table_out, pl.ds(first, HELD)) for first in range(0, BLOCKS, HELD)]
    parts += [(parity, parity_out, pl.ds(0, HELD)), (accum, accum_out, pl.ds(0, BLOCKS))]
    copies = [pltpu.make_async_copy(a.at[part], b.at[part], sem.at[i]) for i, (a, b, part) in enumerate(parts)]
    for copy in copies:
        copy.start()
    for copy in copies:
        copy.wait()


def body(pooled_grad, bag_rows, dest_blocks, block_counts, table, accum, parity, parity_slot):
    hbm = pl.BlockSpec(memory_space=pltpu.HBM)
    vmem = pl.BlockSpec(memory_space=pltpu.VMEM)
    dma = pltpu.SemaphoreType.DMA
    f32, bf16, i32 = jnp.float32, jnp.bfloat16, jnp.int32
    results = ((BLOCKS, BLK, E), (BLOCKS, BLK), (HELD, BLK, E))
    arrays = (
        pooled_grad[0, 0], bag_rows[0, 0], dest_blocks[0, 0].T, block_counts[0],
        table[0, 0], accum[0, 0], parity[0], parity_slot[0],
    )
    updated = pl.pallas_call(
        kernel,
        name="adagrad_step",
        out_shape=[pltpu.VMEM(shape, f32) for shape in results],
        in_specs=[hbm] * len(arrays),
        out_specs=[vmem] * len(results),
        scratch_shapes=[
            pltpu.VMEM((BATCH, E), bf16),
            pltpu.VMEM((OWNERS, CAP, BATCH), i32),
            pltpu.SMEM((CAP, OWNERS), i32),
            pltpu.SMEM((1, OWNERS), i32),
            pltpu.SMEM((1, BLOCKS), i32),
            pltpu.VMEM((BLOCKS, BLK), f32),
            pltpu.VMEM((OWNERS, 1, E), i32),
            pltpu.VMEM((PEERS, 1, E), i32),
            pltpu.VMEM((BLK, BLK), f32),
            pltpu.VMEM((BLK, BLK), f32),
            pltpu.VMEM((1, E), i32),
            pltpu.VMEM((BLOCKS * UNIT, OWNERS * UNIT_TERMS), bf16),
            pltpu.VMEM((2, BLOCKS, WIDE_UNITS * UNIT, E), f32),
            pltpu.VMEM((UNITS, BLOCKS * UNIT, E), bf16),
            pltpu.VMEM((UNITS, CODERS - 1, HELD * UNIT, E), bf16),
            dma((len(arrays) - 1 + len(BAG_PARTS),)),
            dma,
            dma,
            dma((UNITS,)),
            dma((UNITS,)),
            *Stage.scratch_shapes(WIDE_UNITS, WIDE_CHUNKS),
            *Stage.scratch_shapes(THIN_UNITS, THIN_CHUNKS),
        ],
        compiler_params=pltpu.CompilerParams(
            collective_id=0, has_side_effects=True, vmem_limit_bytes=40 * 1024 * 1024
        ),
    )(*[pltpu.with_memory_space_constraint(array, pltpu.HBM) for array in arrays])
    new_table, new_accum, new_parity = pl.pallas_call(
        store,
        name="store_results",
        out_shape=[jax.ShapeDtypeStruct(shape, f32) for shape in results],
        in_specs=[vmem] * len(results),
        out_specs=[hbm] * len(results),
        scratch_shapes=[dma((BLOCKS // HELD + 2,))],
        compiler_params=pltpu.CompilerParams(vmem_limit_bytes=4 * 1024 * 1024),
    )(*updated)
    return (new_table[None, None], new_accum[None, None], new_parity[None])


def solution(mesh):
    placed = (
        P("table", "code", None, None),
        P("table", "code", None, None, None),
        P("table", "code", None, None),
        P("table", "code", None),
        P("table", "code", None, None, None),
        P("table", "code", None, None),
        P("table", "code", None, None),
        P("table", "code", None),
    )
    return jax.shard_map(
        body,
        mesh=mesh,
        in_specs=placed,
        out_specs=(
            P("table", "code", None, None, None),
            P("table", "code", None, None),
            P("table", "code", None, None),
        ),
        check_vma=False,
    )
```

```python
import jax
import jax.numpy as jnp
from jax import lax
from jax.experimental import pallas as pl
from jax.experimental.pallas import tpu as pltpu
from jax.sharding import PartitionSpec as P

LEARN_RATE = 0.2
MESH = pl.DeviceIdType.MESH

RING = 4
CORES = 2
OWNERS = RING * RING * CORES
CODERS = 4
CAP = 4
E = 128
BLK = 128
BLOCKS = 96
HELD = BLOCKS // CODERS
BATCH = 2048

UNIT = 8
UNITS = BLK // UNIT
UNIT_TERMS = CAP * UNIT
WIDE_UNITS, WIDE_CHUNKS = 2, 7
THIN_UNITS, THIN_CHUNKS = 1, 2
CHUNKS = WIDE_CHUNKS + THIN_CHUNKS
DOT_ROWS = 512
LAG = 2


def send_order():
    offsets = [(dz, dx, dc) for dz in range(RING) for dx in range(RING) for dc in range(CORES)][1:]
    offsets.sort(key=lambda m: -(min(m[0], RING - m[0]) + min(m[1], RING - m[1])))
    order = []
    for dz, dx, dc in offsets:
        for _ in range(4):
            if (dz, dx, dc) not in order:
                order.append((dz, dx, dc))
            dz, dx = dx, (RING - dz) % RING
    return order


ORDER = send_order()
BAG_PARTS = [pl.ds(0, OWNERS // 2), pl.ds(OWNERS // 2, OWNERS // 2)]
PEERS = len(ORDER)


class Stage:
    def __init__(self, units, chunks, unit_of, half_of, env, scratch):
        self.units, self.chunks, self.unit_of, self.half_of = units, chunks, unit_of, half_of
        self.env = env
        self.sent, self.received, self.send_sem, self.recv_sem = scratch

    @staticmethod
    def scratch_shapes(units, chunks):
        bf16, dma = jnp.bfloat16, pltpu.SemaphoreType.DMA
        return [
            pltpu.VMEM((chunks, PEERS, units * UNIT_TERMS, E), bf16),
            pltpu.VMEM((chunks, OWNERS, units * UNIT_TERMS, E), bf16),
            dma((chunks,)),
            dma((chunks,)),
        ]

    def send_terms(self, q, before_first_send=None):
        env = self.env
        terms = self.units * UNIT_TERMS
        row_index = lax.broadcasted_iota(jnp.int32, (UNIT, E), 0) + self.unit_of(q) * UNIT
        group = DOT_ROWS // terms
        for start in range(0, OWNERS, group):
            tiles, part = [], []
            for i in range(start, start + group):
                owner = env.owners[i]
                for h in range(self.units):
                    for k in range(CAP):
                        wanted = jnp.where(k < env.counts[0, owner], row_index + h * UNIT, -1)
                        wanted = jnp.concatenate([wanted] * (BATCH // E), axis=1)
                        part.append(jnp.where(env.bags[owner, pl.ds(k, 1), :] == wanted, 1.0, 0.0))
                        if len(part) == 2:
                            tiles.append(jnp.concatenate(part, axis=0).astype(jnp.bfloat16))
                            part = []
            onehot = jnp.concatenate(tiles, axis=0)
            sums = jnp.dot(onehot, env.pooled[...], preferred_element_type=jnp.float32)
            sums = sums.astype(jnp.bfloat16).reshape(group, terms, E)
            if start + group < OWNERS:
                self.sent[q, pl.ds(start, group)] = sums
            else:
                self.sent[q, pl.ds(start, group - 1)] = sums[: group - 1]
                self.received[q, PEERS] = sums[group - 1]
            if self.units == THIN_UNITS:
                self.send(q, start, start + group, before_first_send if start == 0 else None)
        if self.units != THIN_UNITS:
            self.send(q, 0, OWNERS, before_first_send)

    def send(self, q, first, last, before):
        env = self.env
        if before is not None:
            before()
        for i in range(first, min(last, PEERS)):
            pltpu.make_async_remote_copy(
                src_ref=self.sent.at[q, i], dst_ref=self.received.at[q, i],
                send_sem=self.send_sem.at[q], recv_sem=self.recv_sem.at[q],
                device_id=(env.owners[i], env.code), device_id_type=MESH,
            ).start()

    def all_terms(self, q):
        return pltpu.make_async_remote_copy(
            src_ref=self.sent.at[q], dst_ref=self.received.at[q, pl.ds(0, PEERS)],
            send_sem=self.send_sem.at[q], recv_sem=self.recv_sem.at[q],
            device_id=(self.env.me, self.env.code), device_id_type=MESH,
        )

    def combine(self, q):
        env = self.env
        self.all_terms(q).wait_recv()

        def combine_unit(h, carry):
            unit = self.unit_of(q) + h
            first = pl.multiple_of(h * UNIT_TERMS, UNIT_TERMS)
            env.combine_unit(unit, self.half_of(q), h, self.received[q, :, pl.ds(first, UNIT_TERMS), :])
            return carry

        lax.fori_loop(0, self.units, combine_unit, 0)

    def add_blocks(self, q):
        env = self.env
        half = self.half_of(q)
        rows = self.units * UNIT
        first_row = pl.multiple_of(self.unit_of(q) * UNIT, UNIT)

        def add_some(i, carry):
            for j in range(8):
                b = i * 8 + j
                env.table[b, pl.ds(first_row, rows), :] += env.delta[half, env.slots[0, b], pl.ds(0, rows), :]
            return carry

        lax.fori_loop(0, BLOCKS // 8, add_some, 0)

    def finish(self, q):
        def finish_unit(h, carry):
            self.env.finish_unit(self.unit_of(q) + h)
            return carry

        lax.fori_loop(0, self.units, finish_unit, 0)

    def drain(self):
        def wait(q, carry):
            self.all_terms(q).wait_send()
            return carry

        lax.fori_loop(0, self.chunks, wait, 0)


class Env:
    def build_selector(self):
        ids = jnp.concatenate([self.id_recv[i] for i in range(PEERS)] + [self.id_send[PEERS]], axis=0)
        row_in_unit = lax.broadcasted_iota(jnp.int32, (OWNERS, E), 1) % UNIT
        keys = jnp.full((OWNERS, E), -1, jnp.int32)
        for b in range(BLOCKS):
            keys = jnp.where(ids == b, self.slots[0, b] * UNIT + row_in_unit, keys)
        lane = lax.broadcasted_iota(jnp.int32, (1, E), 1)
        per_tile = E // UNIT_TERMS
        lane_tiles = []
        for first in range(0, OWNERS, per_tile):
            tile = keys[first : first + 1, :]
            for j in range(1, per_tile):
                tile = jnp.where(lane >= j * UNIT_TERMS, keys[first + j : first + j + 1, :], tile)
            lane_tiles.append(jnp.broadcast_to(tile, (16, E)))
        row_index = lax.broadcasted_iota(jnp.int32, (16, E), 0)

        def selector_rows(p, carry):
            wanted = row_index + p * 16
            tiles = [jnp.where(tile == wanted, 1.0, 0.0).astype(jnp.bfloat16) for tile in lane_tiles]
            self.selector[pl.ds(pl.multiple_of(p * 16, 16), 16), :] = jnp.concatenate(tiles, axis=1)
            return carry

        lax.fori_loop(0, BLOCKS * UNIT // 16, selector_rows, 0)

    def combine_unit(self, unit, half, h, terms):
        block_rows = pl.ds(pl.multiple_of(unit * UNIT, UNIT), UNIT)
        delta_rows = pl.ds(pl.multiple_of(h * UNIT, UNIT), UNIT)
        terms = terms.reshape(OWNERS * UNIT_TERMS, E)
        old = self.accum_t[block_rows, :] * float(E)
        held_rows = HELD * UNIT
        new_accum = jnp.zeros((UNIT, E), jnp.float32)
        for steps in ((2, 1), (3, 0)):
            copies = []
            for step in steps:
                holder = lax.rem(self.code + step, CODERS)
                span = pl.ds(pl.multiple_of(holder * held_rows, held_rows), held_rows)
                sums = jnp.dot(self.selector[span, :], terms, preferred_element_type=jnp.float32)
                grad = sums.astype(jnp.bfloat16).astype(jnp.float32).reshape(HELD, UNIT, E)
                block = lax.broadcasted_iota(jnp.int32, (HELD, UNIT, E), 0) + holder * HELD
                mine = self.slot_lanes[...].reshape(1, 1, E) == block
                accum = jnp.sum(jnp.where(mine, old[None], 0.0) + grad * grad, axis=-1, keepdims=True) * (1.0 / E)
                change = grad * (-LEARN_RATE * lax.rsqrt(accum))
                new_accum += jnp.sum(jnp.where(mine, accum, 0.0), axis=0)
                self.delta[half, pl.ds(holder * HELD, HELD), delta_rows, :] = change
                if step == 0:
                    self.parity[:, block_rows, :] += change
                else:
                    self.delta_send[unit, span, :] = change.astype(jnp.bfloat16).reshape(held_rows, E)
                    copies.append(
                        pltpu.make_async_remote_copy(
                            src_ref=self.delta_send.at[unit, span], dst_ref=self.delta_recv.at[unit, step - 1],
                            send_sem=self.delta_send_sem.at[unit], recv_sem=self.delta_recv_sem.at[unit],
                            device_id=(self.me, holder), device_id_type=MESH,
                        )
                    )
            for copy in copies:
                copy.start()
        self.new_accum_t[block_rows, :] = new_accum

    def all_deltas(self, unit):
        return pltpu.make_async_remote_copy(
            src_ref=self.delta_recv.at[unit], dst_ref=self.delta_recv.at[unit],
            send_sem=self.delta_send_sem.at[unit], recv_sem=self.delta_recv_sem.at[unit],
            device_id=(self.me, self.code), device_id_type=MESH,
        )

    def finish_unit(self, unit):
        block_rows = pl.ds(pl.multiple_of(unit * UNIT, UNIT), UNIT)
        self.all_deltas(unit).wait_recv()
        total = self.parity[:, block_rows, :]
        for j in range(CODERS - 1):
            total += self.delta_recv[unit, j].astype(jnp.float32).reshape(HELD, UNIT, E)
        self.parity[:, block_rows, :] = total

    def drain(self):
        def wait(unit, carry):
            self.all_deltas(unit).wait_send()
            return carry

        lax.fori_loop(0, UNITS - 1, wait, 0)


def kernel(
    pooled_hbm, bags_hbm, dest_hbm, counts_hbm, table_hbm, accum_hbm, parity_hbm, slots_hbm,
    table, accum_out, parity,
    pooled, bags, dest, counts, slots, accum, id_send, id_recv, accum_t, new_accum_t, slot_lanes,
    selector, delta, delta_send, delta_recv,
    in_sem, id_send_sem, id_recv_sem, delta_send_sem, delta_recv_sem, *stage_scratch,
):
    sources = (counts_hbm, pooled_hbm, *[bags_hbm.at[part] for part in BAG_PARTS], dest_hbm, slots_hbm, accum_hbm, table_hbm, parity_hbm)
    places = (counts, pooled, *[bags.at[part] for part in BAG_PARTS], dest, slots, accum, table, parity)
    loads = [pltpu.make_async_copy(a, b, in_sem.at[i]) for i, (a, b) in enumerate(zip(sources, places))]
    first, second, last = loads[:-5], loads[-5:-2], loads[-2:]
    for load in first:
        load.start()

    me = lax.axis_index("table")
    code = lax.axis_index("code")
    z, x, core = lax.div(me, RING * CORES), lax.rem(lax.div(me, CORES), RING), lax.rem(me, CORES)
    zs = [lax.rem(z + d, RING) * (RING * CORES) for d in range(RING)]
    xs = [lax.rem(x + d, RING) * CORES for d in range(RING)]
    cores = [core, 1 - core]
    owners = [zs[dz] + xs[dx] + cores[dc] for dz, dx, dc in ORDER] + [me]

    env = Env()
    env.me, env.code, env.owners = me, code, owners
    env.pooled, env.bags, env.counts, env.slots = pooled, bags, counts, slots
    env.id_send, env.id_recv, env.accum_t, env.new_accum_t = id_send, id_recv, accum_t, new_accum_t
    env.selector, env.delta, env.delta_send, env.delta_recv = selector, delta, delta_send, delta_recv
    env.delta_send_sem, env.delta_recv_sem = delta_send_sem, delta_recv_sem
    env.table, env.parity, env.slot_lanes = table, parity, slot_lanes
    half = len(stage_scratch) // 2
    wide = Stage(WIDE_UNITS, WIDE_CHUNKS, lambda q: THIN_UNITS + q * WIDE_UNITS, lambda q: lax.rem(q + 1, 2), env, stage_scratch[:half])
    thin = Stage(THIN_UNITS, THIN_CHUNKS, lambda q: q * (UNITS - THIN_UNITS), lambda q: 0, env, stage_scratch[half:])

    def at_chunk(s, do):
        @pl.when((s == 0) | (s == CHUNKS - 1))
        def _():
            do(thin, s // (CHUNKS - 1))

        @pl.when((s > 0) & (s < CHUNKS - 1))
        def _():
            do(wide, s - 1)


    barrier = pltpu.get_barrier_semaphore()
    for owner in owners[:PEERS]:
        pl.semaphore_signal(barrier, inc=1, device_id=(owner, code), device_id_type=MESH)
    for step in range(1, CODERS):
        pl.semaphore_signal(barrier, inc=1, device_id=(me, (code + step) % CODERS), device_id_type=MESH)

    for load in second:
        load.start()
    for load in first:
        load.wait()

    def send_ids():
        lane_slot = (lax.broadcasted_iota(jnp.int32, (1, E), 1) // UNIT) % CAP
        for i, owner in enumerate(owners):
            ids = jnp.full((1, E), -1, jnp.int32)
            for k in range(CAP):
                ids = jnp.where((lane_slot == k) & (k < counts[0, owner]), dest[k, owner], ids)
            id_send[i] = ids
        for i, owner in enumerate(owners[:PEERS]):
            pltpu.make_async_remote_copy(
                src_ref=id_send.at[i], dst_ref=id_recv.at[i], send_sem=id_send_sem, recv_sem=id_recv_sem,
                device_id=(owner, code), device_id_type=MESH,
            ).start()

    def all_ids():
        return pltpu.make_async_remote_copy(
            src_ref=id_send.at[pl.ds(0, PEERS)], dst_ref=id_recv, send_sem=id_send_sem, recv_sem=id_recv_sem,
            device_id=(me, code), device_id_type=MESH,
        )

    def step(s, carry):
        def all_here():
            @pl.when(s == 0)
            def _():
                pl.semaphore_wait(barrier, PEERS + CODERS - 1)

        at_chunk(s, lambda stage, q: stage.send_terms(q, all_here if stage is thin else None))

        @pl.when(s == 0)
        def _():
            for load in last:
                load.start()
            for load in second:
                load.wait()
            send_ids()
            lane = lax.broadcasted_iota(jnp.int32, (1, E), 1)
            lanes = jnp.full((1, E), -1, jnp.int32)
            for b in range(BLOCKS):
                lanes = jnp.where(lane == b, slots[0, b], lanes)
            slot_lanes[...] = lanes
            padding = jnp.zeros((BLK - BLOCKS, BLK), jnp.float32)
            accum_t[...] = jnp.concatenate([accum[...], padding], axis=0).T

        @pl.when(s == 1)
        def _():
            all_ids().wait_recv()
            env.build_selector()
            for load in last:
                load.wait()

        at_chunk(s - LAG, lambda stage, q: stage.combine(q))
        at_chunk(s - LAG - 1, lambda stage, q: stage.add_blocks(q))
        at_chunk(s - LAG - 2, lambda stage, q: stage.finish(q))
        return carry

    lax.fori_loop(0, CHUNKS + LAG + 1, step, 0)
    accum_out[...] = new_accum_t[...].T[:BLOCKS, :]
    all_ids().wait_send()
    wide.drain()
    thin.drain()
    env.drain()
    thin.finish(THIN_CHUNKS - 1)
    env.all_deltas(UNITS - 1).wait_send()


PIECE = 8


def store(table, accum, parity, table_out, accum_out, parity_out, sem):
    parts = [(accum, accum_out, pl.ds(0, BLOCKS))]
    parts += [(parity, parity_out, pl.ds(first, PIECE)) for first in range(0, HELD, PIECE)]
    parts += [(table, table_out, pl.ds(first, PIECE)) for first in range(0, BLOCKS, PIECE)]
    copies = [pltpu.make_async_copy(a.at[part], b.at[part], sem.at[i]) for i, (a, b, part) in enumerate(parts)]
    for copy in copies:
        copy.start()
    for copy in copies:
        copy.wait()


def body(pooled_grad, bag_rows, dest_blocks, block_counts, table, accum, parity, parity_slot):
    hbm = pl.BlockSpec(memory_space=pltpu.HBM)
    vmem = pl.BlockSpec(memory_space=pltpu.VMEM)
    dma = pltpu.SemaphoreType.DMA
    f32, bf16, i32 = jnp.float32, jnp.bfloat16, jnp.int32
    results = ((BLOCKS, BLK, E), (BLOCKS, BLK), (HELD, BLK, E))
    arrays = (
        pooled_grad[0, 0], bag_rows[0, 0], dest_blocks[0, 0].T, block_counts[0],
        table[0, 0], accum[0, 0], parity[0], parity_slot[0],
    )
    updated = pl.pallas_call(
        kernel,
        name="adagrad_step",
        out_shape=[pltpu.VMEM(shape, f32) for shape in results],
        in_specs=[hbm] * len(arrays),
        out_specs=[vmem] * len(results),
        scratch_shapes=[
            pltpu.VMEM((BATCH, E), bf16),
            pltpu.VMEM((OWNERS, CAP, BATCH), i32),
            pltpu.SMEM((CAP, OWNERS), i32),
            pltpu.SMEM((1, OWNERS), i32),
            pltpu.SMEM((1, BLOCKS), i32),
            pltpu.VMEM((BLOCKS, BLK), f32),
            pltpu.VMEM((OWNERS, 1, E), i32),
            pltpu.VMEM((PEERS, 1, E), i32),
            pltpu.VMEM((BLK, BLK), f32),
            pltpu.VMEM((BLK, BLK), f32),
            pltpu.VMEM((1, E), i32),
            pltpu.VMEM((BLOCKS * UNIT, OWNERS * UNIT_TERMS), bf16),
            pltpu.VMEM((2, BLOCKS, WIDE_UNITS * UNIT, E), f32),
            pltpu.VMEM((UNITS, BLOCKS * UNIT, E), bf16),
            pltpu.VMEM((UNITS, CODERS - 1, HELD * UNIT, E), bf16),
            dma((len(arrays) - 1 + len(BAG_PARTS),)),
            dma,
            dma,
            dma((UNITS,)),
            dma((UNITS,)),
            *Stage.scratch_shapes(WIDE_UNITS, WIDE_CHUNKS),
            *Stage.scratch_shapes(THIN_UNITS, THIN_CHUNKS),
        ],
        compiler_params=pltpu.CompilerParams(
            collective_id=0, has_side_effects=True, vmem_limit_bytes=40 * 1024 * 1024
        ),
    )(*[pltpu.with_memory_space_constraint(array, pltpu.HBM) for array in arrays])
    new_table, new_accum, new_parity = pl.pallas_call(
        store,
        name="store_results",
        out_shape=[jax.ShapeDtypeStruct(shape, f32) for shape in results],
        in_specs=[vmem] * len(results),
        out_specs=[hbm] * len(results),
        scratch_shapes=[dma(((BLOCKS + HELD) // PIECE + 1,))],
        compiler_params=pltpu.CompilerParams(vmem_limit_bytes=4 * 1024 * 1024),
    )(*updated)
    return (new_table[None, None], new_accum[None, None], new_parity[None])


def solution(mesh):
    placed = (
        P("table", "code", None, None),
        P("table", "code", None, None, None),
        P("table", "code", None, None),
        P("table", "code", None),
        P("table", "code", None, None, None),
        P("table", "code", None, None),
        P("table", "code", None, None),
        P("table", "code", None),
    )
    return jax.shard_map(
        body,
        mesh=mesh,
        in_specs=placed,
        out_specs=(
            P("table", "code", None, None, None),
            P("table", "code", None, None),
            P("table", "code", None, None),
        ),
        check_vma=False,
    )
```
